32 devices in a mesh: req: 4 (over y, x), mlp: 8 (over z, core).
Axes of the slice: x: 2, y: 2, z: 4, core: 2. Of those that a mesh axis runs over, the one named last changes fastest.
Arguments:
- hidden: bfloat16 [8, 5, 4096], P('req', None, 'mlp'), may hold values from -6 to 6
- attn_gain: float32 [4096], P('mlp'), may hold values from 0.1 to 1.9
- w_qkv: bfloat16 [4096, 6144], P('mlp'), may hold values from -0.09375 to 0.09375
- w_out: bfloat16 [4096, 4096], P(None, 'mlp'), may hold values from -0.09375 to 0.09375
- mlp_gain: float32 [4096], replicated, may hold values from 0.1 to 1.9
- w_gate: bfloat16 [4096, 14336], P(None, ('req', 'mlp')), may hold values from -0.09375 to 0.09375
- w_up: bfloat16 [4096, 14336], P(None, ('req', 'mlp')), may hold values from -0.09375 to 0.09375
- w_down: bfloat16 [14336, 4096], P(('req', 'mlp')), may hold values from -0.09375 to 0.09375
- kv_cache: bfloat16 [8, 1024, 2048], P('req', 'mlp')
- lengths: int32 [8], P('req'), may hold values from 1 to 1024, as said below
- mig_slot: int32 [4], replicated, may hold values from 0 to 1, as said below
- mig_dest: int32 [4], replicated, may hold values from 0 to 3, each once
Outputs:
- layer_out: bfloat16 [8, 5, 4096], P('req', None, 'mlp')
- moved_cache: bfloat16 [4, 128, 2048], P('req', 'mlp')
The draws below stay inside these ranges and needn't reach their ends.
Inputs may be any that keep to these rules, and one draw needn't show every extreme that they name: `mig_slot`: the slot of each group that its leaving request vacates and the arriving one takes. `mig_dest`: A permutation of the groups: every group receives exactly one request. `lengths`: in slot g * 2 + mig_slot[g] the length is at most 128, reached in some group; some slot has exactly 1024.
All inputs are finite; a program needn't handle non-finite values.
Results may differ from the reference program's by a relative error of at most 0.012.
The reference program's roundings to bfloat16 on the way count: a program that leaves them out, or rounds other values in their place, can miss the bound.
Values may be sent and summed in bfloat16 or wider, within the bound.
A program may use at most 128 MiB of HBM per device.

```python
import jax
import jax.numpy as jnp
from jax import lax

D = 4096
HEADS = 32
KVH = 8
HD = 128
FF = 14336
R_DEV = 2
CTX_DEV = 128
SPEC = 5
MIG_ROWS = 16
GROUPS = 4
SLOTS = 8
CTX = 1024
MIG_CTX = 128
TOKENS = 40
N_MLP = 8


def slot_plan(key):
    folded = jax.random.fold_in(key, 11)
    slot_key, long_key, short_key = jax.random.split(folded, 3)
    arriving = jax.random.randint(slot_key, (GROUPS,), 0, R_DEV)
    span_rows = jax.random.randint(long_key, (GROUPS, R_DEV), 1, CTX + 1)
    shorter = jax.random.randint(short_key, (GROUPS,), 1, MIG_CTX + 1)
    marked = jnp.arange(R_DEV)[None, :] == arriving[:, None]
    span_rows = jnp.where(marked, shorter[:, None], span_rows)
    span_rows = span_rows.at[0, arriving[0]].set(MIG_CTX)
    span_rows = span_rows.at[0, (arriving[0] + 1) % R_DEV].set(CTX)
    return (arriving.astype(jnp.int32), span_rows.reshape(SLOTS).astype(jnp.int32))


def draw_mig_slot(key, part):
    return slot_plan(key)[0]


def draw_lengths(key, part):
    return slot_plan(key)[1]


def draw_kv_cache(key, part):
    kv_width = KVH * HD
    entries = jax.random.normal(key, (SLOTS, CTX, 2 * kv_width), jnp.float32)
    return entries.astype(jnp.bfloat16)


def raised(array, key, source, target, shards_of, factor):
    owner, partner = [(jnp.arange(array.shape[dim]) // (array.shape[dim] // shards_of)).reshape([-1 if axis == dim else 1 for axis in range(array.ndim)]) for dim in (source, target)]
    chosen = jax.random.permutation(key, shards_of)[partner]
    strong = (owner == chosen) | (owner == (partner + shards_of // 2) % shards_of)
    return jnp.where(strong, factor * array, array)


def level_of(rng, extent, cuts, smallest, high):
    def one(dim, shards_of):
        heights = jax.random.uniform(jax.random.fold_in(jax.random.fold_in(rng, 6), dim), (shards_of,), jnp.float32, smallest / len(cuts), high / len(cuts))
        return jnp.repeat(jnp.exp(heights), extent[dim] // shards_of).reshape((-1,) + (1,) * (len(extent) - dim - 1))

    gain = one(*cuts[0])
    for cut in cuts[1:]:
        gain = gain * one(*cut)
    return gain


def bell_draw(key, shape, deviation, limit, shards=(), kind=jnp.bfloat16):
    drawn = jax.random.normal(key, shape, jnp.float32) * deviation
    if len(shards) > 0:
        drawn = level_of(key, shape, shards, -0.22, 0.18) * drawn
    return jnp.clip(drawn, min=-limit, max=limit).astype(kind)


def gaussian_with(key, shape, width, limit, cuts, heavy, kind=jnp.bfloat16):
    drawn = width * jax.random.normal(key, shape, jnp.float32)
    if cuts:
        drawn = drawn * level_of(key, shape, cuts, -0.22, 0.18)
    return jnp.clip(raised(drawn, jax.random.fold_in(key, 3), *heavy), -limit, limit).astype(kind)


def setup_inputs(seed: int = 0) -> dict:
    key_of = jax.random.split(jax.random.key(seed), 13)
    return {
        "hidden": bell_draw(key_of[0], (SLOTS, SPEC, D), 1.0, 6.0, ((0, 4), (2, 8))),
        "attn_gain": jnp.clip(1.0 + 0.18 * jax.random.normal(key_of[1], (D,), jnp.float32), 0.1, 1.9),
        "w_qkv": bell_draw(key_of[2], (D, HEADS * HD + 2 * KVH * HD), D ** -0.5, 0.09375, ((0, 8),)),
        "w_out": bell_draw(key_of[3], (HEADS * HD, D), (HEADS * HD) ** -0.5, 0.09375, ((1, 8),)),
        "mlp_gain": jnp.clip(1.0 + 0.18 * jax.random.normal(key_of[4], (D,), jnp.float32), 0.1, 1.9),
        "w_gate": bell_draw(key_of[5], (D, FF), D ** -0.5, 0.09375, ((1, 32),)),
        "w_up": bell_draw(key_of[6], (D, FF), D ** -0.5, 0.09375, ((1, 32),)),
        "w_down": gaussian_with(key_of[7], (FF, D), FF ** -0.5, 0.09375, ((0, 32),), (0, 1, 32, 2.75)),
        "kv_cache": draw_kv_cache(jax.random.fold_in(key_of[12], 71), 0),
        "lengths": draw_lengths(jax.random.fold_in(key_of[12], 71), 0),
        "mig_slot": draw_mig_slot(jax.random.fold_in(key_of[12], 71), 0),
        "mig_dest": jax.random.permutation(key_of[11], GROUPS).astype(jnp.int32),
    }


EPSILON = 1e-05
ROPE_BASE = 500000.0
NEG_FILL = -1e+30

def rotate(vectors, positions):
    half_dim = vectors.shape[-1] // 2
    frequency = ROPE_BASE ** (-(jnp.arange(half_dim).astype(jnp.float32) / half_dim))
    angles = positions.astype(jnp.float32)[..., None, None] * frequency
    cos_part = jnp.cos(angles)
    sin_part = jnp.sin(angles)
    leading = vectors[..., :half_dim]
    trailing = vectors[..., half_dim:]
    return jnp.concatenate([leading * cos_part - trailing * sin_part, trailing * cos_part + leading * sin_part], axis=-1)

def combine(former, latter):
    former_max, former_sum, former_acc = former
    latter_max, latter_sum, latter_acc = latter
    highest = jnp.maximum(former_max, latter_max)
    former_rate = jnp.exp(former_max - highest)
    latter_rate = jnp.exp(latter_max - highest)
    return (highest, former_sum * former_rate + latter_sum * latter_rate, former_acc * former_rate[..., None] + latter_acc * latter_rate[..., None])

def softmax_part(scores, usable, values, pattern):
    highest = lax.optimization_barrier(jnp.max(jnp.where(usable, scores, NEG_FILL), axis=-1))
    weights = jnp.where(usable, jnp.exp(scores - highest[..., None]), 0.0)
    rounded = weights.astype(jnp.bfloat16).astype(jnp.float32)
    return (highest, lax.optimization_barrier(jnp.sum(weights, axis=-1)), jnp.einsum(pattern, rounded, values))

def reference(hidden, attn_gain, w_qkv, w_out, mlp_gain, w_gate, w_up, w_down, kv_cache, lengths, mig_slot, mig_dest):
    kv_width = KVH * HD
    full_width = 2 * kv_width
    blocks = kv_cache.reshape(GROUPS, R_DEV, N_MLP, CTX_DEV, full_width)
    source = jnp.zeros((GROUPS,), jnp.int32).at[mig_dest].set(jnp.arange(GROUPS, dtype=jnp.int32))
    moving = blocks[source, mig_slot[source], :, :MIG_ROWS]
    blocks = blocks.at[jnp.arange(GROUPS, dtype=jnp.int32), mig_slot, :, :MIG_ROWS].set(moving)
    moved_cache = moving.reshape(GROUPS, MIG_CTX, full_width)
    live_cache = blocks.reshape(SLOTS, N_MLP, CTX_DEV, full_width)
    widened = hidden.astype(jnp.float32)
    inverse = lax.rsqrt(lax.optimization_barrier(jnp.sum(widened * widened, axis=-1)) / D + EPSILON)
    scaled = (widened * attn_gain).astype(jnp.bfloat16)
    projected = jnp.dot(scaled.reshape(TOKENS, D), w_qkv, preferred_element_type=jnp.float32)
    projected = projected.reshape(SLOTS, SPEC, -1) * inverse[..., None]
    positions = lengths[:, None] + jnp.arange(SPEC, dtype=jnp.int32)[None, :]
    query_width = HEADS * HD
    queries = rotate(projected[..., :query_width].reshape(SLOTS, SPEC, HEADS, HD), positions).astype(jnp.bfloat16)
    new_keys = rotate(projected[..., query_width:query_width + kv_width].reshape(SLOTS, SPEC, KVH, HD), positions).astype(jnp.bfloat16)
    new_values = projected[..., query_width + kv_width:].reshape(SLOTS, SPEC, KVH, HD).astype(jnp.bfloat16)
    grouped = queries.reshape(SLOTS, SPEC, KVH, HEADS // KVH, HD).astype(jnp.float32)
    score_scale = HD ** (-0.5)
    running = None
    for block_id in range(N_MLP):
        block_kv = live_cache[:, block_id]
        key_rows = block_kv[..., :kv_width].reshape(SLOTS, CTX_DEV, KVH, HD).astype(jnp.float32)
        value_rows = block_kv[..., kv_width:].reshape(SLOTS, CTX_DEV, KVH, HD).astype(jnp.float32)
        scores = jnp.einsum('rsgqd,rcgd->rgsqc', grouped, key_rows) * score_scale
        position = jnp.arange(CTX_DEV, dtype=jnp.int32) * N_MLP + block_id
        usable = (position[None, :] < lengths[:, None])[:, None, None, None, :]
        current = softmax_part(scores, usable, value_rows, 'rgsqc,rcgd->rgsqd')
        running = current if running is None else combine(running, current)
    own_scores = jnp.einsum('rsgqd,rtgd->rgsqt', grouped, new_keys.astype(jnp.float32)) * score_scale
    causal = (jnp.arange(SPEC)[:, None] >= jnp.arange(SPEC)[None, :])[None, None, :, None, :]
    own_part = softmax_part(own_scores, causal, new_values.astype(jnp.float32), 'rgsqt,rtgd->rgsqd')
    highest, summed, mixture = combine(running, own_part)
    attended = (mixture / summed[..., None]).transpose(0, 2, 1, 3, 4).reshape(SLOTS, SPEC, query_width).astype(jnp.bfloat16)
    residual = (widened + jnp.dot(attended.reshape(TOKENS, query_width), w_out, preferred_element_type=jnp.float32).reshape(SLOTS, SPEC, D)).astype(jnp.bfloat16)
    residual_rows = residual.astype(jnp.float32).reshape(TOKENS, D)
    inverse_m = lax.rsqrt(lax.optimization_barrier(jnp.sum(residual_rows * residual_rows, axis=-1)) / D + EPSILON)
    scaled_m = (residual_rows * mlp_gain).astype(jnp.bfloat16)
    gate_proj = jnp.dot(scaled_m, w_gate, preferred_element_type=jnp.float32) * inverse_m[:, None]
    up_proj = jnp.dot(scaled_m, w_up, preferred_element_type=jnp.float32) * inverse_m[:, None]
    activated = (jax.nn.silu(gate_proj) * up_proj).astype(jnp.bfloat16)
    layer_out = (residual_rows + jnp.dot(activated, w_down, preferred_element_type=jnp.float32)).astype(jnp.bfloat16)
    return (layer_out.reshape(SLOTS, SPEC, D), moved_cache)
```

```python
import functools

import jax
import jax.numpy as jnp
import numpy as np
from jax import lax
from jax.experimental import pallas as pl
from jax.experimental.pallas import tpu as pltpu
from jax.sharding import PartitionSpec as P

HEADS = 32
KVH = 8
HD = 128
MIG_ROWS = 16
EPSILON = 1e-05
ROPE_BASE = 500000.0
NEG_FILL = -1e30
SLOT_ROWS = 8
ROWS = 16
F32 = jnp.float32
BF16 = jnp.bfloat16


def aligned(index, multiple):
    return pl.multiple_of(index, multiple)


def loop(start, stop, step):
    def lap(k, carry):
        step(k)
        return carry

    lax.fori_loop(start, stop, lap, 0)


def dot(a, b):
    return jnp.dot(a, b, preferred_element_type=F32)


def dot_t(a, b):
    return lax.dot_general(a, b, (((1,), (1,)), ((), ())), preferred_element_type=F32)


def softmax_part(queries, keys, values, usable):
    scores = dot_t(queries, keys) * (HD ** (-0.5))
    highest = jnp.max(jnp.where(usable, scores, NEG_FILL), axis=-1, keepdims=True)
    weights = jnp.where(usable, jnp.exp(scores - highest), 0.0)
    return highest, jnp.sum(weights, axis=-1, keepdims=True), dot(weights.astype(BF16), values)


def stat_rows(highest, summed):
    rows = highest.shape[0]
    lane = lax.broadcasted_iota(jnp.int32, (rows, 128), 1)
    wide = jnp.where(lane % 2 == 0, highest, summed)
    if rows < 128:
        wide = jnp.concatenate([wide, jnp.zeros((128 - rows, 128), F32)], axis=0)
    return jnp.transpose(wide)[:8]


def kernel(
    G,
    B,
    spec_len,
    lengths,
    mig_slot,
    mig_dest,
    freq,
    hidden_h,
    again_h,
    wqkv_h,
    wout_h,
    mgain_h,
    wgate_h,
    wup_h,
    wdown_h,
    kv_h,
    out,
    moved_h,
    hid,
    again,
    wqkv,
    wout,
    mgain,
    wgate,
    wup,
    wdown,
    kv,
    xs,
    kvp,
    p_send,
    p_recv,
    mig_send,
    mig_recv,
    moved,
    q_all,
    acc_send,
    acc_recv,
    st_send,
    st_recv,
    rates,
    att_all,
    res_all,
    act,
    d_send,
    d_recv,
    e_send,
    e_recv,
    ld_sem,
    p_ss,
    p_rs,
    m_ss,
    m_rs,
    q_ss,
    q_rs,
    a_ss,
    a_rs,
    t_ss,
    t_rs,
    o_ss,
    o_rs,
    r_ss,
    r_rs,
    f_ss,
    f_rs,
    d_ss,
    d_rs,
    e_ss,
    e_rs,
):
    me_r = lax.axis_index("req")
    me_b = lax.axis_index("mlp")
    W = hid.shape[2]
    D = W * B
    QW = HEADS * HD // B
    HQ = HEADS // B
    REP = B // KVH
    SR = HQ * SLOT_ROWS
    RQ = 2 * SR
    KV0 = HEADS * HD

    def peer_b(j):
        return lax.rem(me_b + j, B)

    def from_b(j):
        return lax.rem(me_b + B - j, B)

    def peer_r(j):
        return lax.rem(me_r + j, G)

    def from_r(j):
        return lax.rem(me_r + G - j, G)

    def to_mlp(src, dst, ss, rs, j):
        return pltpu.make_async_remote_copy(
            src_ref=src, dst_ref=dst, send_sem=ss, recv_sem=rs,
            device_id={"mlp": peer_b(j)}, device_id_type=pl.DeviceIdType.MESH,
        )

    def to_req(src, dst, ss, rs, j):
        return pltpu.make_async_remote_copy(
            src_ref=src, dst_ref=dst, send_sem=ss, recv_sem=rs,
            device_id={"req": peer_r(j)}, device_id_type=pl.DeviceIdType.MESH,
        )

    loads = [
        pltpu.make_async_copy(src, dst, ld_sem.at[i])
        for i, (src, dst) in enumerate(
            [
                (hidden_h, hid),
                (again_h, again),
                (wqkv_h, wqkv),
                (kv_h, kv),
                (wout_h, wout),
                (mgain_h, mgain),
                (wgate_h, wgate),
                (wup_h, wup),
                (wdown_h, wdown),
            ]
        )
    ]
    for load in loads[:4]:
        load.start()

    barrier = pltpu.get_barrier_semaphore()
    for j in range(1, B):
        pl.semaphore_signal(
            barrier, inc=1, device_id={"mlp": peer_b(j)}, device_id_type=pl.DeviceIdType.MESH
        )
    for j in range(1, G):
        pl.semaphore_signal(
            barrier, inc=1, device_id={"req": peer_r(j)}, device_id_type=pl.DeviceIdType.MESH
        )

    xs[...] = jnp.zeros_like(xs)
    loads[0].wait()
    loads[1].wait()
    for t in range(spec_len):
        both = hid[t].astype(F32)
        for s in range(2):
            xs[s * SLOT_ROWS + t : s * SLOT_ROWS + t + 1, :] = both[s : s + 1]
    x = xs[...]
    square = jnp.sum(x * x, axis=-1, keepdims=True)
    scaled = (x * again[...]).astype(BF16)
    lane = lax.broadcasted_iota(jnp.int32, (ROWS, 128), 1)
    high = jnp.broadcast_to(square, (ROWS, 128)).astype(BF16).astype(F32)
    square_cols = jnp.where(lane < 64, high, square - high).astype(BF16)
    loads[2].wait()
    for load in loads[4:]:
        load.start()
    kvp[...] = dot(scaled, wqkv[:, KV0:]).astype(BF16)

    def project(d, slot):
        head = lax.div(d, REP)
        p_send[slot, :, :QW] = dot(scaled, wqkv[:, pl.ds(aligned(d * QW, 128), QW)]).astype(BF16)
        p_send[slot, :, QW : QW + HD] = kvp[:, pl.ds(aligned(head * HD, 128), HD)]
        p_send[slot, :, QW + HD : QW + 2 * HD] = kvp[:, pl.ds(aligned((KVH + head) * HD, 128), HD)]
        p_send[slot, :, QW + 2 * HD :] = square_cols

    def p_copy(j):
        return to_mlp(p_send.at[j], p_recv.at[j], p_ss.at[j], p_rs.at[j], j)

    pl.semaphore_wait(barrier, B + G - 2)

    def p_step(j):
        project(peer_b(j), j)
        p_copy(j).start()

    loop(1, B, p_step)
    project(me_b, 0)

    loads[3].wait()
    own_slot = mig_slot[me_r]
    kv_w = kv.shape[2]
    slot_of = jnp.full((MIG_ROWS, kv_w), own_slot, jnp.int32)
    leaving = jnp.where(
        slot_of == 0, kv[0, :MIG_ROWS, :].astype(F32), kv[1, :MIG_ROWS, :].astype(F32)
    )
    mig_send[...] = leaving.astype(BF16)

    def m_copy(j):
        return to_req(mig_send, mig_recv.at[j], m_ss.at[j], m_rs.at[j], j)

    for j in range(1, G):
        m_copy(j).start()

    row = lax.broadcasted_iota(jnp.int32, (ROWS, 128), 0)
    first = row < SLOT_ROWS
    position = jnp.where(
        first, jnp.full((ROWS, 128), lengths[0], jnp.int32) + row,
        jnp.full((ROWS, 128), lengths[1], jnp.int32) + (row - SLOT_ROWS),
    )
    angle = position.astype(F32) * freq[...]
    cos_part = jnp.cos(angle)
    sin_part = jnp.where(lane < HD // 2, -jnp.sin(angle), jnp.sin(angle))

    def rotate(v):
        return v * cos_part + pltpu.roll(v, HD // 2, 1) * sin_part

    total = p_send[0].astype(F32)
    for j in range(1, B):
        p_copy(j).wait_recv()
        total = total + p_recv[j].astype(F32)
    last = total[:, QW + 2 * HD :]
    square_sum = jnp.sum(
        jnp.where((lane == 0) | (lane == 64), last, 0.0), axis=-1, keepdims=True
    )
    projected = total[:, : QW + 2 * HD] * lax.rsqrt(square_sum / D + EPSILON)
    heads = [rotate(projected[:, n * HD : (n + 1) * HD]) for n in range(HQ)]
    own_q = jnp.concatenate(
        [
            heads[n][s * SLOT_ROWS : (s + 1) * SLOT_ROWS]
            for s in range(2)
            for n in range(HQ)
        ],
        axis=0,
    ).astype(BF16)
    q_all[me_b] = own_q

    def q_copy(j):
        return to_mlp(q_all.at[me_b], q_all.at[me_b], q_ss.at[j], q_rs.at[j], j)

    def q_arrival(j):
        b = from_b(j)
        return to_mlp(q_all.at[b], q_all.at[b], q_ss.at[j], q_rs.at[j], j)

    for j in range(1, B):
        q_copy(j).start()

    pad = jnp.zeros((128 - ROWS, HD), F32)
    new_k = jnp.concatenate([rotate(projected[:, QW : QW + HD]), pad], axis=0).astype(BF16)
    new_v = jnp.concatenate([projected[:, QW + HD :], pad], axis=0).astype(BF16)
    r_i = lax.broadcasted_iota(jnp.int32, (RQ, 128), 0)
    c_i = lax.broadcasted_iota(jnp.int32, (RQ, 128), 1)
    same = (r_i // SR) == (c_i // SLOT_ROWS)
    causal = same & ((c_i % SLOT_ROWS) <= (r_i % SLOT_ROWS))
    own_max, own_sum, own_acc = softmax_part(own_q, new_k, new_v, causal)
    own_stats = stat_rows(own_max, own_sum)

    arrived = jnp.where(
        jnp.full((MIG_ROWS, kv_w), mig_dest[me_r], jnp.int32) == me_r,
        mig_send[...].astype(F32), 0.0,
    )
    for j in range(1, G):
        m_copy(j).wait_recv()
        arrived = jnp.where(
            jnp.full((MIG_ROWS, kv_w), mig_dest[from_r(j)], jnp.int32) == me_r,
            mig_recv[j].astype(F32), arrived,
        )
    moved[0] = arrived.astype(BF16)
    moved_copy = pltpu.make_async_copy(moved, moved_h, ld_sem.at[len(loads)])
    moved_copy.start()
    for s in range(2):
        kv[s, :MIG_ROWS, :] = jnp.where(
            slot_of == s, arrived, kv[s, :MIG_ROWS, :].astype(F32)
        ).astype(BF16)

    stored = lax.broadcasted_iota(jnp.int32, (SR, kv.shape[1]), 1) * B + me_b
    usable = [stored < jnp.full(stored.shape, lengths[s], jnp.int32) for s in range(2)]

    def attend(b, slot):
        head = lax.div(b, REP)
        k_at = pl.ds(aligned(head * HD, 128), HD)
        v_at = pl.ds(aligned((KVH + head) * HD, 128), HD)
        q = q_all[b]
        parts = [
            softmax_part(q[s * SR : (s + 1) * SR], kv[s, :, k_at], kv[s, :, v_at], usable[s])
            for s in range(2)
        ]
        high_c, sum_c, acc = [
            jnp.concatenate([parts[0][i], parts[1][i]], axis=0) for i in range(3)
        ]
        acc_send[slot] = acc.astype(BF16)
        st_send[slot] = stat_rows(high_c, sum_c)

    def a_copy(j):
        return pltpu.make_async_remote_copy(
            src_ref=acc_send.at[j], dst_ref=acc_recv.at[j], send_sem=a_ss.at[j],
            recv_sem=a_rs.at[j], device_id={"mlp": from_b(j)},
            device_id_type=pl.DeviceIdType.MESH,
        )

    def t_copy(j):
        return pltpu.make_async_remote_copy(
            src_ref=st_send.at[j], dst_ref=st_recv.at[j], send_sem=t_ss.at[j],
            recv_sem=t_rs.at[j], device_id={"mlp": from_b(j)},
            device_id_type=pl.DeviceIdType.MESH,
        )

    def a_step(j):
        q_arrival(j).wait_recv()
        attend(from_b(j), j)
        a_copy(j).start()
        t_copy(j).start()

    loop(1, B, a_step)
    attend(me_b, 0)

    stats = [own_stats, st_send[0]]
    for j in range(1, B):
        t_copy(j).wait_recv()
        stats.append(st_recv[j])
    top = functools.reduce(jnp.maximum, [s[0:1] for s in stats])
    scales = [jnp.exp(s[0:1] - top) for s in stats]
    summed = functools.reduce(jnp.add, [e * s[1:2] for e, s in zip(scales, stats)])
    rates[...] = jnp.zeros_like(rates)
    for i, e in enumerate(scales):
        rates[i : i + 1, :] = e / summed
    columns = jnp.transpose(rates[...])
    mixture = own_acc * columns[:RQ, 0:1] + acc_send[0].astype(F32) * columns[:RQ, 1:2]
    for j in range(1, B):
        a_copy(j).wait_recv()
        mixture = mixture + acc_recv[j].astype(F32) * columns[:RQ, j + 1 : j + 2]
    attended = jnp.concatenate(
        [
            jnp.concatenate(
                [
                    mixture[s * SR + n * SLOT_ROWS : s * SR + (n + 1) * SLOT_ROWS]
                    for s in range(2)
                ],
                axis=0,
            )
            for n in range(HQ)
        ],
        axis=1,
    ).astype(BF16)
    att_all[0] = attended

    def o_copy(j):
        return to_mlp(att_all.at[0], att_all.at[j], o_ss.at[j], o_rs.at[j], j)

    for j in range(1, B):
        o_copy(j).start()

    loads[4].wait()

    def out_part(b, slot):
        return dot(att_all[slot], wout[pl.ds(aligned(b * QW, 128), QW), :])

    def o_step(j, so_far):
        o_copy(j).wait_recv()
        return so_far + out_part(from_b(j), j)

    attn_out = lax.fori_loop(1, B, o_step, out_part(me_b, 0))
    residual = (xs[...] + attn_out).astype(BF16)

    res_all[me_r, me_b] = residual

    def r_copy(j):
        here = res_all.at[me_r, me_b]
        return to_mlp(here, here, r_ss.at[j], r_rs.at[j], j)

    def r_arrival(j):
        here = res_all.at[me_r, from_b(j)]
        return to_mlp(here, here, r_ss.at[j], r_rs.at[j], j)

    def f_copy(i, j, b):
        here = res_all.at[me_r, b]
        return to_req(here, here, f_ss.at[i, j], f_rs.at[i, j], i)

    def f_arrival(i, j):
        here = res_all.at[from_r(i), from_b(j)]
        return to_req(here, here, f_ss.at[i, j], f_rs.at[i, j], i)

    for j in range(1, B):
        r_copy(j).start()
    for i in range(1, G):
        f_copy(i, 0, me_b).start()

    def f_step(j):
        r_arrival(j).wait_recv()
        for i in range(1, G):
            f_copy(i, j, from_b(j)).start()

    loop(1, B, f_step)

    loads[5].wait()
    loads[6].wait()
    loads[7].wait()
    M = G * ROWS
    F = wgate.shape[0]

    def up_step(j, carry):
        sq, gate, up = carry
        b = from_b(j)
        block = res_all[:, b].reshape(M, W).astype(F32)
        sq = sq + jnp.sum(block * block, axis=-1, keepdims=True)
        rows = (block * mgain[:, pl.ds(aligned(b * W, 128), W)]).astype(BF16)
        depth = pl.ds(aligned(b * W, 128), W)
        return sq, gate + dot_t(rows, wgate[:, depth]), up + dot_t(rows, wup[:, depth])

    def up_lap(j, carry):
        for i in range(1, G):
            f_arrival(i, j).wait_recv()
        return up_step(j, carry)

    zero = jnp.zeros((M, F), F32)
    sq, gate, up = lax.fori_loop(0, B, up_lap, (jnp.zeros((M, 1), F32), zero, zero))
    inverse = lax.rsqrt(sq / D + EPSILON)
    gate = gate * inverse
    up = up * inverse
    act[...] = (gate / (1.0 + jnp.exp(-gate)) * up).astype(BF16)

    loads[8].wait()

    def d_copy(i, j):
        return to_req(
            d_send.at[j, peer_r(i)], d_recv.at[j, i], d_ss.at[i, j], d_rs.at[i, j], i
        )

    def d_step(k):
        j = lax.rem(k + 1, B)
        b = peer_b(j)
        part = dot(act[...], wdown[:, pl.ds(aligned(b * W, 128), W)])
        d_send[j] = part.astype(BF16).reshape(G, ROWS, W)
        for i in range(1, G):
            d_copy(i, j).start()

    loop(0, B, d_step)

    def e_copy(j):
        return to_mlp(e_send.at[j], e_recv.at[j], e_ss.at[j], e_rs.at[j], j)

    def summed_block(j):
        so_far = d_send[j, me_r].astype(F32)
        for i in range(1, G):
            d_copy(i, j).wait_recv()
            so_far = so_far + d_recv[j, i].astype(F32)
        return so_far

    def e_step(j):
        e_send[j] = summed_block(j).astype(BF16)
        e_copy(j).start()

    loop(1, B, e_step)
    result = res_all[me_r, me_b].astype(F32) + summed_block(0)
    for j in range(1, B):
        e_copy(j).wait_recv()
        result = result + e_recv[j].astype(F32)
    for t in range(spec_len):
        out[t] = jnp.concatenate(
            [result[s * SLOT_ROWS + t : s * SLOT_ROWS + t + 1] for s in range(2)], axis=0
        ).astype(BF16)

    moved_copy.wait()
    for j in range(1, G):
        m_copy(j).wait_send()

    def drain(j):
        p_copy(j).wait_send()
        q_copy(j).wait_send()
        a_copy(j).wait_send()
        t_copy(j).wait_send()
        o_copy(j).wait_send()
        r_copy(j).wait_send()
        e_copy(j).wait_send()

    loop(1, B, drain)

    def drain_req(j):
        for i in range(1, G):
            f_copy(i, j, from_b(j)).wait_send()
            d_copy(i, j).wait_send()

    loop(0, B, drain_req)


def body(
    hidden, attn_gain, w_qkv, w_out, mlp_gain, w_gate, w_up, w_down,
    kv_cache, lengths, mig_slot, mig_dest,
):
    G = lax.axis_size("req")
    B = lax.axis_size("mlp")
    slots, spec_len, W = hidden.shape
    QW = HEADS * HD // B
    RQ = 2 * (HEADS // B) * SLOT_ROWS
    CW = QW + 3 * HD
    kv_w = kv_cache.shape[2]
    F = w_gate.shape[1]
    w_gate, w_up = w_gate.T, w_up.T
    hidden = hidden.transpose(1, 0, 2)
    half = HD // 2
    freq = np.float32(ROPE_BASE) ** (-(np.arange(half, dtype=np.float32) / np.float32(half)))
    freq = jnp.asarray(np.concatenate([freq, freq])[None, :], F32)
    anywhere = pl.BlockSpec(memory_space=pl.ANY)
    smem = pl.BlockSpec(memory_space=pltpu.SMEM)
    vmem = pl.BlockSpec(memory_space=pltpu.VMEM)
    V = pltpu.VMEM
    dma = pltpu.SemaphoreType.DMA
    scratch = [
        V(hidden.shape, BF16),
        V((1, W), F32),
        V(w_qkv.shape, BF16),
        V(w_out.shape, BF16),
        V((1, mlp_gain.shape[0]), F32),
        V(w_gate.shape, BF16),
        V(w_up.shape, BF16),
        V(w_down.shape, BF16),
        V(kv_cache.shape, BF16),
        V((ROWS, W), F32),
        V((ROWS, kv_w), BF16),
        V((B, ROWS, CW), BF16),
        V((B, ROWS, CW), BF16),
        V((MIG_ROWS, kv_w), BF16),
        V((G, MIG_ROWS, kv_w), BF16),
        V((1, MIG_ROWS, kv_w), BF16),
        V((B, RQ, HD), BF16),
        V((B, RQ, HD), BF16),
        V((B, RQ, HD), BF16),
        V((B, 8, 128), F32),
        V((B, 8, 128), F32),
        V((128, 128), F32),
        V((B, ROWS, QW), BF16),
        V((G, B, ROWS, W), BF16),
        V((G * ROWS, F), BF16),
        V((B, G, ROWS, W), BF16),
        V((B, G, ROWS, W), BF16),
        V((B, ROWS, W), BF16),
        V((B, ROWS, W), BF16),
        dma((10,)),
        dma((B,)), dma((B,)),
        dma((G,)), dma((G,)),
        dma((B,)), dma((B,)),
        dma((B,)), dma((B,)),
        dma((B,)), dma((B,)),
        dma((B,)), dma((B,)),
        dma((B,)), dma((B,)),
        dma((G, B)), dma((G, B)),
        dma((G, B)), dma((G, B)),
        dma((B,)), dma((B,)),
    ]
    layer_out, moved = pl.pallas_call(
        functools.partial(kernel, G, B, spec_len),
        out_shape=(
            jax.ShapeDtypeStruct(hidden.shape, BF16),
            jax.ShapeDtypeStruct((1, MIG_ROWS, kv_w), BF16),
        ),
        in_specs=[smem, smem, smem, vmem] + [anywhere] * 9,
        out_specs=(vmem, anywhere),
        scratch_shapes=scratch,
        compiler_params=pltpu.CompilerParams(
            collective_id=0, has_side_effects=True, vmem_limit_bytes=56 * 1024 * 1024
        ),
    )(
        lengths, mig_slot, mig_dest, freq, hidden, attn_gain.reshape(1, W), w_qkv, w_out,
        mlp_gain.reshape(1, -1), w_gate, w_up, w_down, kv_cache,
    )
    return layer_out.transpose(1, 0, 2), moved


def solution(mesh):
    placed = (
        P("req", None, "mlp"),
        P("mlp"),
        P("mlp", None),
        P(None, "mlp"),
        P(),
        P(None, ("req", "mlp")),
        P(None, ("req", "mlp")),
        P(("req", "mlp"), None),
        P("req", "mlp", None),
        P("req"),
        P(),
        P(),
    )
    return jax.shard_map(
        body,
        mesh=mesh,
        in_specs=placed,
        out_specs=(P("req", None, "mlp"), P("req", "mlp", None)),
        check_vma=False,
    )
```

```python
import functools

import jax
import jax.numpy as jnp
import numpy as np
from jax import lax
from jax.experimental import pallas as pl
from jax.experimental.pallas import tpu as pltpu
from jax.sharding import PartitionSpec as P

HEADS = 32
KVH = 8
HD = 128
MIG_ROWS = 16
EPSILON = 1e-05
ROPE_BASE = 500000.0
NEG_FILL = -1e30
SLOT_ROWS = 8
ROWS = 16
F32 = jnp.float32
BF16 = jnp.bfloat16


def aligned(index, multiple):
    return pl.multiple_of(index, multiple)


def loop(start, stop, step):
    def lap(k, carry):
        step(k)
        return carry

    lax.fori_loop(start, stop, lap, 0)


def dot(a, b):
    return jnp.dot(a, b, preferred_element_type=F32)


def dot_t(a, b):
    return lax.dot_general(a, b, (((1,), (1,)), ((), ())), preferred_element_type=F32)


def softmax_part(queries, keys, values, usable):
    scores = dot_t(queries, keys) * (HD ** (-0.5))
    highest = jnp.max(jnp.where(usable, scores, NEG_FILL), axis=-1, keepdims=True)
    weights = jnp.where(usable, jnp.exp(scores - highest), 0.0)
    return highest, jnp.sum(weights, axis=-1, keepdims=True), dot(weights.astype(BF16), values)


def stat_rows(highest, summed):
    rows = highest.shape[0]
    lane = lax.broadcasted_iota(jnp.int32, (rows, 128), 1)
    wide = jnp.where(lane % 2 == 0, highest, summed)
    if rows < 128:
        wide = jnp.concatenate([wide, jnp.zeros((128 - rows, 128), F32)], axis=0)
    return jnp.transpose(wide)[:8]


def kernel(
    G,
    B,
    spec_len,
    lengths,
    mig_slot,
    mig_dest,
    freq,
    hidden_h,
    again_h,
    wqkv_h,
    wout_h,
    mgain_h,
    wgate_h,
    wup_h,
    wdown_h,
    kv_h,
    out,
    moved_h,
    hid,
    again,
    wqkv,
    wout,
    mgain,
    wgate,
    wup,
    wdown,
    kv,
    xs,
    kvp,
    p_send,
    p_recv,
    mig_send,
    mig_recv,
    moved,
    q_all,
    acc_send,
    acc_recv,
    st_send,
    st_recv,
    rates,
    att_all,
    res_all,
    act,
    c_send,
    c_recv,
    d_own,
    d_send,
    d_recv,
    e_send,
    e_recv,
    ld_sem,
    p_ss,
    p_rs,
    m_ss,
    m_rs,
    q_ss,
    q_rs,
    a_ss,
    a_rs,
    t_ss,
    t_rs,
    o_ss,
    o_rs,
    r_ss,
    r_rs,
    f_ss,
    f_rs,
    s_ss,
    s_rs,
    c_ss,
    c_rs,
    d_ss,
    d_rs,
    e_ss,
    e_rs,
):
    me_r = lax.axis_index("req")
    me_b = lax.axis_index("mlp")
    W = hid.shape[2]
    D = W * B
    QW = HEADS * HD // B
    HQ = HEADS // B
    REP = B // KVH
    SR = HQ * SLOT_ROWS
    RQ = 2 * SR
    KV0 = HEADS * HD

    def peer_b(j):
        return lax.rem(me_b + j, B)

    def from_b(j):
        return lax.rem(me_b + B - j, B)

    def peer_r(j):
        return lax.rem(me_r + j, G)

    def from_r(j):
        return lax.rem(me_r + G - j, G)

    def to_mlp(src, dst, ss, rs, j):
        return pltpu.make_async_remote_copy(
            src_ref=src, dst_ref=dst, send_sem=ss, recv_sem=rs,
            device_id={"mlp": peer_b(j)}, device_id_type=pl.DeviceIdType.MESH,
        )

    def to_req(src, dst, ss, rs, j):
        return pltpu.make_async_remote_copy(
            src_ref=src, dst_ref=dst, send_sem=ss, recv_sem=rs,
            device_id={"req": peer_r(j)}, device_id_type=pl.DeviceIdType.MESH,
        )

    loads = [
        pltpu.make_async_copy(src, dst, ld_sem.at[i])
        for i, (src, dst) in enumerate(
            [
                (hidden_h, hid),
                (again_h, again),
                (wqkv_h, wqkv),
                (kv_h, kv),
                (wout_h, wout),
                (mgain_h, mgain),
                (wgate_h, wgate),
                (wup_h, wup),
                (wdown_h, wdown),
            ]
        )
    ]
    for load in loads[:4]:
        load.start()

    barrier = pltpu.get_barrier_semaphore()
    for j in range(1, B):
        pl.semaphore_signal(
            barrier, inc=1, device_id={"mlp": peer_b(j)}, device_id_type=pl.DeviceIdType.MESH
        )
    for j in range(1, G):
        pl.semaphore_signal(
            barrier, inc=1, device_id={"req": peer_r(j)}, device_id_type=pl.DeviceIdType.MESH
        )

    xs[...] = jnp.zeros_like(xs)
    loads[0].wait()
    loads[1].wait()
    for t in range(spec_len):
        both = hid[t].astype(F32)
        for s in range(2):
            xs[s * SLOT_ROWS + t : s * SLOT_ROWS + t + 1, :] = both[s : s + 1]
    x = xs[...]
    square = jnp.sum(x * x, axis=-1, keepdims=True)
    scaled = (x * again[...]).astype(BF16)
    lane = lax.broadcasted_iota(jnp.int32, (ROWS, 128), 1)
    high = jnp.broadcast_to(square, (ROWS, 128)).astype(BF16).astype(F32)
    square_cols = jnp.where(lane < 64, high, square - high).astype(BF16)
    loads[2].wait()
    for load in loads[4:]:
        load.start()
    kvp[...] = dot(scaled, wqkv[:, KV0:]).astype(BF16)

    def project(d, slot):
        head = lax.div(d, REP)
        p_send[slot, :, :QW] = dot(scaled, wqkv[:, pl.ds(aligned(d * QW, 128), QW)]).astype(BF16)
        p_send[slot, :, QW : QW + HD] = kvp[:, pl.ds(aligned(head * HD, 128), HD)]
        p_send[slot, :, QW + HD : QW + 2 * HD] = kvp[:, pl.ds(aligned((KVH + head) * HD, 128), HD)]
        p_send[slot, :, QW + 2 * HD :] = square_cols

    def p_copy(j):
        return to_mlp(p_send.at[j], p_recv.at[j], p_ss.at[j], p_rs.at[j], j)

    pl.semaphore_wait(barrier, B + G - 2)

    def p_step(j):
        project(peer_b(j), j)
        p_copy(j).start()

    loop(1, B, p_step)
    project(me_b, 0)

    loads[3].wait()
    own_slot = mig_slot[me_r]
    kv_w = kv.shape[2]
    slot_of = jnp.full((MIG_ROWS, kv_w), own_slot, jnp.int32)
    leaving = jnp.where(
        slot_of == 0, kv[0, :MIG_ROWS, :].astype(F32), kv[1, :MIG_ROWS, :].astype(F32)
    )
    mig_send[...] = leaving.astype(BF16)

    def m_copy(j):
        return to_req(mig_send, mig_recv.at[j], m_ss.at[j], m_rs.at[j], j)

    for j in range(1, G):
        m_copy(j).start()

    row = lax.broadcasted_iota(jnp.int32, (ROWS, 128), 0)
    first = row < SLOT_ROWS
    position = jnp.where(
        first, jnp.full((ROWS, 128), lengths[0], jnp.int32) + row,
        jnp.full((ROWS, 128), lengths[1], jnp.int32) + (row - SLOT_ROWS),
    )
    angle = position.astype(F32) * freq[...]
    cos_part = jnp.cos(angle)
    sin_part = jnp.where(lane < HD // 2, -jnp.sin(angle), jnp.sin(angle))

    def rotate(v):
        return v * cos_part + pltpu.roll(v, HD // 2, 1) * sin_part

    total = p_send[0].astype(F32)
    for j in range(1, B):
        p_copy(j).wait_recv()
        total = total + p_recv[j].astype(F32)
    last = total[:, QW + 2 * HD :]
    square_sum = jnp.sum(
        jnp.where((lane == 0) | (lane == 64), last, 0.0), axis=-1, keepdims=True
    )
    projected = total[:, : QW + 2 * HD] * lax.rsqrt(square_sum / D + EPSILON)
    heads = [rotate(projected[:, n * HD : (n + 1) * HD]) for n in range(HQ)]
    own_q = jnp.concatenate(
        [
            heads[n][s * SLOT_ROWS : (s + 1) * SLOT_ROWS]
            for s in range(2)
            for n in range(HQ)
        ],
        axis=0,
    ).astype(BF16)
    q_all[me_b] = own_q

    def q_copy(j):
        return to_mlp(q_all.at[me_b], q_all.at[me_b], q_ss.at[j], q_rs.at[j], j)

    def q_arrival(j):
        b = from_b(j)
        return to_mlp(q_all.at[b], q_all.at[b], q_ss.at[j], q_rs.at[j], j)

    for j in range(1, B):
        q_copy(j).start()

    pad = jnp.zeros((128 - ROWS, HD), F32)
    new_k = jnp.concatenate([rotate(projected[:, QW : QW + HD]), pad], axis=0).astype(BF16)
    new_v = jnp.concatenate([projected[:, QW + HD :], pad], axis=0).astype(BF16)
    r_i = lax.broadcasted_iota(jnp.int32, (RQ, 128), 0)
    c_i = lax.broadcasted_iota(jnp.int32, (RQ, 128), 1)
    same = (r_i // SR) == (c_i // SLOT_ROWS)
    causal = same & ((c_i % SLOT_ROWS) <= (r_i % SLOT_ROWS))
    own_max, own_sum, own_acc = softmax_part(own_q, new_k, new_v, causal)
    own_stats = stat_rows(own_max, own_sum)

    arrived = jnp.where(
        jnp.full((MIG_ROWS, kv_w), mig_dest[me_r], jnp.int32) == me_r,
        mig_send[...].astype(F32), 0.0,
    )
    for j in range(1, G):
        m_copy(j).wait_recv()
        arrived = jnp.where(
            jnp.full((MIG_ROWS, kv_w), mig_dest[from_r(j)], jnp.int32) == me_r,
            mig_recv[j].astype(F32), arrived,
        )
    moved[0] = arrived.astype(BF16)
    moved_copy = pltpu.make_async_copy(moved, moved_h, ld_sem.at[len(loads)])
    moved_copy.start()
    for s in range(2):
        kv[s, :MIG_ROWS, :] = jnp.where(
            slot_of == s, arrived, kv[s, :MIG_ROWS, :].astype(F32)
        ).astype(BF16)

    stored = lax.broadcasted_iota(jnp.int32, (SR, kv.shape[1]), 1) * B + me_b
    usable = [stored < jnp.full(stored.shape, lengths[s], jnp.int32) for s in range(2)]

    def attend(b, slot):
        head = lax.div(b, REP)
        k_at = pl.ds(aligned(head * HD, 128), HD)
        v_at = pl.ds(aligned((KVH + head) * HD, 128), HD)
        q = q_all[b]
        parts = [
            softmax_part(q[s * SR : (s + 1) * SR], kv[s, :, k_at], kv[s, :, v_at], usable[s])
            for s in range(2)
        ]
        high_c, sum_c, acc = [
            jnp.concatenate([parts[0][i], parts[1][i]], axis=0) for i in range(3)
        ]
        acc_send[slot] = acc.astype(BF16)
        st_send[slot] = stat_rows(high_c, sum_c)

    def a_copy(j):
        return pltpu.make_async_remote_copy(
            src_ref=acc_send.at[j], dst_ref=acc_recv.at[j], send_sem=a_ss.at[j],
            recv_sem=a_rs.at[j], device_id={"mlp": from_b(j)},
            device_id_type=pl.DeviceIdType.MESH,
        )

    def t_copy(j):
        return pltpu.make_async_remote_copy(
            src_ref=st_send.at[j], dst_ref=st_recv.at[j], send_sem=t_ss.at[j],
            recv_sem=t_rs.at[j], device_id={"mlp": from_b(j)},
            device_id_type=pl.DeviceIdType.MESH,
        )

    def a_step(j):
        q_arrival(j).wait_recv()
        attend(from_b(j), j)
        a_copy(j).start()
        t_copy(j).start()

    loop(1, B, a_step)
    attend(me_b, 0)

    stats = [own_stats, st_send[0]]
    for j in range(1, B):
        t_copy(j).wait_recv()
        stats.append(st_recv[j])
    top = functools.reduce(jnp.maximum, [s[0:1] for s in stats])
    scales = [jnp.exp(s[0:1] - top) for s in stats]
    summed = functools.reduce(jnp.add, [e * s[1:2] for e, s in zip(scales, stats)])
    rates[...] = jnp.zeros_like(rates)
    for i, e in enumerate(scales):
        rates[i : i + 1, :] = e / summed
    columns = jnp.transpose(rates[...])
    mixture = own_acc * columns[:RQ, 0:1] + acc_send[0].astype(F32) * columns[:RQ, 1:2]
    for j in range(1, B):
        a_copy(j).wait_recv()
        mixture = mixture + acc_recv[j].astype(F32) * columns[:RQ, j + 1 : j + 2]
    attended = jnp.concatenate(
        [
            jnp.concatenate(
                [
                    mixture[s * SR + n * SLOT_ROWS : s * SR + (n + 1) * SLOT_ROWS]
                    for s in range(2)
                ],
                axis=0,
            )
            for n in range(HQ)
        ],
        axis=1,
    ).astype(BF16)
    att_all[0] = attended

    def o_copy(j):
        return to_mlp(att_all.at[0], att_all.at[j], o_ss.at[j], o_rs.at[j], j)

    for j in range(1, B):
        o_copy(j).start()

    loads[4].wait()

    def out_part(b, slot):
        return dot(att_all[slot], wout[pl.ds(aligned(b * QW, 128), QW), :])

    def o_step(j, so_far):
        o_copy(j).wait_recv()
        return so_far + out_part(from_b(j), j)

    attn_out = lax.fori_loop(1, B, o_step, out_part(me_b, 0))
    residual = (xs[...] + attn_out).astype(BF16)

    Z = B // 2
    core = lax.rem(me_b, 2)
    my_z = lax.div(me_b, 2)
    sibling = my_z * 2 + (1 - core)

    def peer_z(j):
        return lax.rem(my_z + j, Z) * 2 + core

    def from_z(j):
        return lax.rem(my_z + Z - j, Z) * 2 + core

    def other_core(b):
        return b + 1 - 2 * core

    def to_b(src, dst, ss, rs, b):
        return pltpu.make_async_remote_copy(
            src_ref=src, dst_ref=dst, send_sem=ss, recv_sem=rs,
            device_id={"mlp": b}, device_id_type=pl.DeviceIdType.MESH,
        )

    res_all[me_r, me_b] = residual

    def r_copy(j):
        here = res_all.at[me_r, me_b]
        return to_b(here, here, r_ss.at[j], r_rs.at[j], peer_z(j))

    def r_arrival(j):
        here = res_all.at[me_r, from_z(j)]
        return to_b(here, here, r_ss.at[j], r_rs.at[j], peer_z(j))

    def f_copy(i, j):
        here = res_all.at[me_r, from_z(j)]
        return to_req(here, here, f_ss.at[i, j], f_rs.at[i, j], i)

    def f_arrival(i, j):
        here = res_all.at[from_r(i), from_z(j)]
        return to_req(here, here, f_ss.at[i, j], f_rs.at[i, j], i)

    def s_copy(i, j):
        here = res_all.at[from_r(i), from_z(j)]
        return to_b(here, here, s_ss.at[i, j], s_rs.at[i, j], sibling)

    def s_arrival(i, j):
        here = res_all.at[from_r(i), other_core(from_z(j))]
        return to_b(here, here, s_ss.at[i, j], s_rs.at[i, j], sibling)

    for j in range(1, Z):
        r_copy(j).start()
    for i in range(1, G):
        f_copy(i, 0).start()
    s_copy(0, 0).start()

    def f_step(j):
        r_arrival(j).wait_recv()
        for i in range(1, G):
            f_copy(i, j).start()
        s_copy(0, j).start()

    loop(1, Z, f_step)

    loads[5].wait()
    loads[6].wait()
    loads[7].wait()
    M = G * ROWS
    F = wgate.shape[0]

    def up_step(b, carry):
        sq, gate, up = carry
        block = res_all[:, b].reshape(M, W).astype(F32)
        sq = sq + jnp.sum(block * block, axis=-1, keepdims=True)
        depth = pl.ds(aligned(b * W, 128), W)
        rows = (block * mgain[:, depth]).astype(BF16)
        return sq, gate + dot_t(rows, wgate[:, depth]), up + dot_t(rows, wup[:, depth])

    def up_lap(j, carry):
        for i in range(1, G):
            f_arrival(i, j).wait_recv()
            s_copy(i, j).start()
        return up_step(from_z(j), carry)

    def up_lap_other(j, carry):
        for i in range(G):
            s_arrival(i, j).wait_recv()
        return up_step(other_core(from_z(j)), carry)

    zero = jnp.zeros((M, F), F32)
    sums = lax.fori_loop(0, Z, up_lap, (jnp.zeros((M, 1), F32), zero, zero))
    sq, gate, up = lax.fori_loop(0, Z, up_lap_other, sums)
    inverse = lax.rsqrt(sq / D + EPSILON)
    gate = gate * inverse
    up = up * inverse
    act[...] = (gate / (1.0 + jnp.exp(-gate)) * up).astype(BF16)

    loads[8].wait()

    def down_part(b):
        return dot(act[...], wdown[:, pl.ds(aligned(b * W, 128), W)])

    def c_copy(j):
        return to_b(c_send.at[j], c_recv.at[j], c_ss.at[j], c_rs.at[j], sibling)

    def c_step(k):
        j = lax.rem(k + 1, Z)
        c_send[j] = down_part(other_core(peer_z(j)))
        c_copy(j).start()

    loop(0, Z, c_step)

    def d_copy(i, j):
        return to_req(
            d_send.at[j, peer_r(i)], d_recv.at[j, i], d_ss.at[i, j], d_rs.at[i, j], i
        )

    def d_step(k):
        j = lax.rem(k + 1, Z)
        part = down_part(peer_z(j))
        c_copy(j).wait_recv()
        part = (part + c_recv[j]).reshape(G, ROWS, W)
        d_own[j] = part
        d_send[j] = part.astype(BF16)
        for i in range(1, G):
            d_copy(i, j).start()

    loop(0, Z, d_step)

    def e_copy(j):
        return to_b(e_send.at[j], e_recv.at[j], e_ss.at[j], e_rs.at[j], peer_z(j))

    def summed_block(j):
        so_far = d_own[j, me_r]
        for i in range(1, G):
            d_copy(i, j).wait_recv()
            so_far = so_far + d_recv[j, i].astype(F32)
        return so_far

    def e_step(j):
        e_send[j] = summed_block(j).astype(BF16)
        e_copy(j).start()

    loop(1, Z, e_step)
    result = res_all[me_r, me_b].astype(F32) + summed_block(0)
    for j in range(1, Z):
        e_copy(j).wait_recv()
        result = result + e_recv[j].astype(F32)
    for t in range(spec_len):
        out[t] = jnp.concatenate(
            [result[s * SLOT_ROWS + t : s * SLOT_ROWS + t + 1] for s in range(2)], axis=0
        ).astype(BF16)

    moved_copy.wait()
    for j in range(1, G):
        m_copy(j).wait_send()

    def drain(j):
        p_copy(j).wait_send()
        q_copy(j).wait_send()
        a_copy(j).wait_send()
        t_copy(j).wait_send()
        o_copy(j).wait_send()

    loop(1, B, drain)

    def drain_z(j):
        r_copy(j).wait_send()
        e_copy(j).wait_send()

    loop(1, Z, drain_z)

    def drain_req(j):
        c_copy(j).wait_send()
        s_copy(0, j).wait_send()
        for i in range(1, G):
            f_copy(i, j).wait_send()
            s_copy(i, j).wait_send()
            d_copy(i, j).wait_send()

    loop(0, Z, drain_req)


def body(
    hidden, attn_gain, w_qkv, w_out, mlp_gain, w_gate, w_up, w_down,
    kv_cache, lengths, mig_slot, mig_dest,
):
    G = lax.axis_size("req")
    B = lax.axis_size("mlp")
    Z = B // 2
    slots, spec_len, W = hidden.shape
    QW = HEADS * HD // B
    RQ = 2 * (HEADS // B) * SLOT_ROWS
    CW = QW + 3 * HD
    kv_w = kv_cache.shape[2]
    F = w_gate.shape[1]
    w_gate, w_up = w_gate.T, w_up.T
    hidden = hidden.transpose(1, 0, 2)
    half = HD // 2
    freq = np.float32(ROPE_BASE) ** (-(np.arange(half, dtype=np.float32) / np.float32(half)))
    freq = jnp.asarray(np.concatenate([freq, freq])[None, :], F32)
    anywhere = pl.BlockSpec(memory_space=pl.ANY)
    smem = pl.BlockSpec(memory_space=pltpu.SMEM)
    vmem = pl.BlockSpec(memory_space=pltpu.VMEM)
    V = pltpu.VMEM
    dma = pltpu.SemaphoreType.DMA
    scratch = [
        V(hidden.shape, BF16),
        V((1, W), F32),
        V(w_qkv.shape, BF16),
        V(w_out.shape, BF16),
        V((1, mlp_gain.shape[0]), F32),
        V(w_gate.shape, BF16),
        V(w_up.shape, BF16),
        V(w_down.shape, BF16),
        V(kv_cache.shape, BF16),
        V((ROWS, W), F32),
        V((ROWS, kv_w), BF16),
        V((B, ROWS, CW), BF16),
        V((B, ROWS, CW), BF16),
        V((MIG_ROWS, kv_w), BF16),
        V((G, MIG_ROWS, kv_w), BF16),
        V((1, MIG_ROWS, kv_w), BF16),
        V((B, RQ, HD), BF16),
        V((B, RQ, HD), BF16),
        V((B, RQ, HD), BF16),
        V((B, 8, 128), F32),
        V((B, 8, 128), F32),
        V((128, 128), F32),
        V((B, ROWS, QW), BF16),
        V((G, B, ROWS, W), BF16),
        V((G * ROWS, F), BF16),
        V((Z, G * ROWS, W), F32),
        V((Z, G * ROWS, W), F32),
        V((Z, G, ROWS, W), F32),
        V((Z, G, ROWS, W), BF16),
        V((Z, G, ROWS, W), BF16),
        V((Z, ROWS, W), BF16),
        V((Z, ROWS, W), BF16),
        dma((10,)),
        dma((B,)), dma((B,)),
        dma((G,)), dma((G,)),
        dma((B,)), dma((B,)),
        dma((B,)), dma((B,)),
        dma((B,)), dma((B,)),
        dma((B,)), dma((B,)),
        dma((Z,)), dma((Z,)),
        dma((G, Z)), dma((G, Z)),
        dma((G, Z)), dma((G, Z)),
        dma((Z,)), dma((Z,)),
        dma((G, Z)), dma((G, Z)),
        dma((Z,)), dma((Z,)),
    ]
    layer_out, moved = pl.pallas_call(
        functools.partial(kernel, G, B, spec_len),
        out_shape=(
            jax.ShapeDtypeStruct(hidden.shape, BF16),
            jax.ShapeDtypeStruct((1, MIG_ROWS, kv_w), BF16),
        ),
        in_specs=[smem, smem, smem, vmem] + [anywhere] * 9,
        out_specs=(vmem, anywhere),
        scratch_shapes=scratch,
        compiler_params=pltpu.CompilerParams(
            collective_id=0, has_side_effects=True, vmem_limit_bytes=56 * 1024 * 1024
        ),
    )(
        lengths, mig_slot, mig_dest, freq, hidden, attn_gain.reshape(1, W), w_qkv, w_out,
        mlp_gain.reshape(1, -1), w_gate, w_up, w_down, kv_cache,
    )
    return layer_out.transpose(1, 0, 2), moved


def solution(mesh):
    placed = (
        P("req", None, "mlp"),
        P("mlp"),
        P("mlp", None),
        P(None, "mlp"),
        P(),
        P(None, ("req", "mlp")),
        P(None, ("req", "mlp")),
        P(("req", "mlp"), None),
        P("req", "mlp", None),
        P("req"),
        P(),
        P(),
    )
    return jax.shard_map(
        body,
        mesh=mesh,
        in_specs=placed,
        out_specs=(P("req", None, "mlp"), P("req", "mlp", None)),
        check_vma=False,
    )
```
